256 devices in a mesh: freq: 8 (over x, z_hi), row: 8 (over z_lo, core), col: 4 (over y).
Axes of the slice: x: 4, y: 4, z: 8 (z_hi: 2, z_lo: 4; z = z_hi * 4 + z_lo), core: 2. Of those that a mesh axis runs over, the one named last changes fastest.
Arguments:
- traces: bfloat16 [512, 1024, 2048], P(('col', 'row', 'freq')), may hold values from -6 to 6
- band_bins: int32 [256], replicated, may hold values from 1 to 1023
- panel_start: int32 [8], replicated, may hold values from 0 to 7, as said below
Outputs:
- multiples: bfloat16 [2, 256, 1024, 512], P(None, 'freq', 'row', 'col')
The draws below stay inside these ranges and needn't reach their ends.
Inputs may be any that keep to these rules, and one draw needn't show every extreme that they name: Step n's panel covers shot and receiver indices panel_start[n] * 64 to panel_start[n] * 64 + 63; panels may repeat, and some may be absent.
All inputs are finite; a program needn't handle non-finite values.
Results may differ from the reference program's by a relative error of at most 0.0066.
Values may be sent and summed in bfloat16 or wider, within the bound.
A program may use at most 64 MiB of HBM per device.

```python
import math
import jax
import jax.numpy as jnp
from jax import lax

NT = 2048
PANEL = 64
PANELS = 8
NF = 256
NR = 1024
NS = 512


def draw_panel_start(key, part):
    key = jax.random.fold_in(key, 7)
    pick_key, place_key = jax.random.split(key)
    chosen = jax.random.randint(pick_key, (PANELS,), 0, PANELS).astype(jnp.int32)
    places = jax.random.permutation(place_key, PANELS)
    chosen = chosen.at[places[0]].set(0)
    chosen = chosen.at[places[1]].set(PANELS - 1)
    return chosen.astype(jnp.int32)


def plant(entries, stream_key, least, top_value):
    extent = entries.shape
    index_at = [jax.random.randint(jax.random.fold_in(stream_key, axis), (), 0, extent[axis]) for axis in range(len(extent))]
    entries = entries.at[tuple(index_at)].set(least)
    longest = extent.index(max(extent))
    index_at[longest] = (index_at[longest] + 1) % extent[longest]
    return entries.at[tuple(index_at)].set(top_value)


def shard_levels(stream_key, dims, pieces, least, high):
    gain = 1.0
    for position, blocks in pieces:
        steps = jax.random.uniform(jax.random.fold_in(jax.random.fold_in(stream_key, 6), position), (blocks,), jnp.float32, least / len(pieces), high / len(pieces))
        gain = gain * jnp.repeat(jnp.exp(steps), dims[position] // blocks).reshape((-1,) + (1,) * (len(dims) - 1 - position))
    return gain


def bell_draw(own_key, extent, scale, bound, shards=(), kind=jnp.bfloat16):
    values = jax.random.normal(own_key, extent, jnp.float32) * scale
    if len(shards) > 0:
        values = shard_levels(own_key, extent, shards, -0.22, 0.18) * values
    return jnp.clip(values, min=-bound, max=bound).astype(kind)


def setup_inputs(seed: int = 0) -> dict:
    keys = jax.random.split(jax.random.key(seed), 4)
    traces = bell_draw(keys[0], (NS, NR, NT), 1.0, 6.0, ((0, 256),))
    band_bins = plant(jax.random.randint(keys[1], (NF,), 1, NT // 2), jax.random.fold_in(keys[1], 1), 1, (NT // 2) - 1).astype(jnp.int32)
    panel_start = draw_panel_start(jax.random.fold_in(keys[3], 71), 0)
    return {"traces": traces, "band_bins": band_bins, "panel_start": panel_start}


def dft_table(band_bins):
    times = jnp.arange(NT, dtype=jnp.int32)
    wrapped = times[:, None] * band_bins[None, :].astype(jnp.int32) % NT
    angles = wrapped.astype(jnp.float32) * (2.0 * math.pi / NT)
    stacked = jnp.stack([jnp.cos(angles), -jnp.sin(angles)], axis=1)
    return stacked.reshape(NT, 2 * NF).astype(jnp.bfloat16)

def reference(traces, band_bins, panel_start):
    flat_table = dft_table(band_bins)
    inverse_root = 1.0 / math.sqrt(NT)

    def transform(gather_rows):
        return (jnp.dot(gather_rows, flat_table, preferred_element_type=jnp.float32) * inverse_root).astype(jnp.bfloat16)
    spectra = lax.map(transform, traces)
    spectra = spectra.reshape(NS, NR, 2, NF).transpose(2, 3, 1, 0)
    starts = panel_start.astype(jnp.int32) * PANEL
    left_panels = jnp.concatenate([lax.dynamic_slice_in_dim(spectra, starts[n], PANEL, 3) for n in range(PANELS)], axis=3)
    right_panels = jnp.concatenate([lax.dynamic_slice_in_dim(spectra, starts[n], PANEL, 2) for n in range(PANELS)], axis=2)
    out_scale = 1.0 / math.sqrt(PANELS * PANEL)

    def per_frequency(operands):
        left_part, right_part = operands
        real_part = jnp.dot(left_part[0], right_part[0], preferred_element_type=jnp.float32) - jnp.dot(left_part[1], right_part[1], preferred_element_type=jnp.float32)
        imag_part = jnp.dot(left_part[0], right_part[1], preferred_element_type=jnp.float32) + jnp.dot(left_part[1], right_part[0], preferred_element_type=jnp.float32)
        return (jnp.stack([real_part, imag_part]) * out_scale).astype(jnp.bfloat16)
    result = lax.map(per_frequency, (left_panels.transpose(1, 0, 2, 3), right_panels.transpose(1, 0, 2, 3)))
    return result.transpose(1, 0, 2, 3)
```

```python
import math

import jax
import jax.numpy as jnp
from jax import lax
from jax.sharding import PartitionSpec as P

PANEL = 64


def build_table(band_bins, samples):
    times = jnp.arange(samples, dtype=jnp.int32)
    wrapped = band_bins[:, None] * times[None, :] % samples
    angles = wrapped.astype(jnp.float32) * (2.0 * math.pi / samples)
    return jnp.stack([jnp.cos(angles), -jnp.sin(angles)], axis=1).astype(jnp.bfloat16)


def on_device(traces, band_bins, panel_start):
    own_shots, receivers, samples = traces.shape
    freqs, rows, cols = (lax.axis_size(n) for n in ("freq", "row", "col"))
    devices = freqs * rows * cols
    shots = own_shots * devices
    panels = panel_start.shape[0]
    bins = band_bins.reshape(freqs, cols, rows).transpose(1, 2, 0).reshape(devices)
    table = build_table(bins, samples).reshape(2 * devices, samples)
    flat = traces.reshape(own_shots * receivers, samples)
    spectrum = lax.dot_general(
        table, flat, (((1,), (1,)), ((), ())), preferred_element_type=jnp.float32
    )
    spectrum = (spectrum * (1.0 / math.sqrt(samples))).astype(jnp.bfloat16)
    spectrum = spectrum.reshape(devices, 2, own_shots, receivers)
    received = lax.all_to_all(
        spectrum, ("col", "row", "freq"), split_axis=0, concat_axis=0, tiled=True
    )
    field = received.transpose(1, 0, 2, 3).reshape(2, shots, receivers)
    starts = panel_start * PANEL
    first = jnp.concatenate(
        [lax.dynamic_slice_in_dim(field, starts[n], PANEL, 1) for n in range(panels)], axis=1
    )
    second = jnp.concatenate(
        [lax.dynamic_slice_in_dim(field, starts[n], PANEL, 2) for n in range(panels)], axis=2
    )

    def product(p, q):
        return lax.dot_general(
            first[p], second[q], (((0,), (1,)), ((), ())), preferred_element_type=jnp.float32
        )

    scale = 1.0 / math.sqrt(panels * PANEL)
    real = (product(0, 0) - product(1, 1)) * scale
    imag = (product(0, 1) + product(1, 0)) * scale
    out = jnp.stack([real, imag]).astype(jnp.bfloat16)
    out = out.reshape(2, rows, receivers // rows, cols, shots // cols)
    out = out.transpose(3, 1, 0, 2, 4).reshape(cols * rows, 2, receivers // rows, shots // cols)
    out = lax.all_to_all(out, ("col", "row"), split_axis=0, concat_axis=0, tiled=True)
    return out.transpose(1, 0, 2, 3)


def solution(mesh):
    return jax.shard_map(
        on_device,
        mesh=mesh,
        in_specs=(P(("col", "row", "freq"), None, None), P(), P()),
        out_specs=P(None, "freq", "row", "col"),
        check_vma=False,
    )
```

```python
import functools
import math

import jax
import jax.numpy as jnp
from jax import lax
from jax.experimental import pallas as pl
from jax.experimental.pallas import tpu as pltpu
from jax.sharding import PartitionSpec as P

PANEL = 64
MESH = pl.DeviceIdType.MESH
BF16 = jnp.bfloat16
F32 = jnp.float32


def iota(shape, dim):
    return lax.broadcasted_iota(jnp.int32, shape, dim)


def dot(a, b):
    return lax.dot_general(a, b, (((1,), (0,)), ((), ())), preferred_element_type=F32)


def dot_t(a, b):
    return lax.dot_general(a, b, (((1,), (1,)), ((), ())), preferred_element_type=F32)


def cos_sin(phase):
    quadrant = ((phase + 256) >> 9) & 3
    rest = (phase - 512 * ((phase + 256) >> 9)).astype(F32) * (2.0 * math.pi / 2048)
    square = rest * rest
    sine = rest * (1.0 + square * (-1.0 / 6 + square * (1.0 / 120 + square * (-1.0 / 5040 + square * (1.0 / 362880)))))
    cosine = 1.0 + square * (-0.5 + square * (1.0 / 24 + square * (-1.0 / 720 + square * (1.0 / 40320 - square * (1.0 / 3628800)))))
    odd = (quadrant & 1) == 1
    first, second = jnp.where(odd, sine, cosine), jnp.where(odd, cosine, sine)
    first = jnp.where((quadrant == 1) | (quadrant == 2), -first, first)
    second = jnp.where(quadrant >= 2, -second, second)
    return first, second


def kernel(bins, starts, traces, out, x_buf, table, tiles, send, received, field, left, blocks, chosen,
           load_sem, send_sem, recv_sem, own_sem, ready_sem):
    f, r, y = (lax.axis_index(n) for n in ("freq", "row", "col"))
    x, zh, zl, core = f // 2, f % 2, r // 2, r % 2
    z = zh * 4 + zl

    def device(x, y, z, core):
        return (x * 2 + z // 4, z % 4 * 2 + core, y)

    def load(n):
        return pltpu.make_async_copy(
            traces.at[n // 4, pl.ds(n % 4 * 256, 256)], x_buf.at[pl.ds(n * 256, 256)], load_sem.at[n]
        )

    for n in range(8):
        load(n).start()

    barrier = pltpu.get_barrier_semaphore()

    def along_z(k):
        return device(x, y, (z + k // 2) % 8, (core + k % 2) % 2)

    def along_xy(k):
        return device((x + k // 4) % 4, (y + k % 4) % 4, z, core)

    def greet(k, _):
        pl.semaphore_signal(barrier, inc=1, device_id=along_z(k), device_id_type=MESH)
        pl.semaphore_signal(barrier, inc=1, device_id=along_xy(k), device_id_type=MESH)
        return 0

    lax.fori_loop(1, 16, greet, 0)

    row, col = iota((256, 256), 0), iota((256, 256), 1)
    outward = (col == (row & 15) * 16 + ((row >> 4) & 1) * 8 + (row >> 5)).astype(BF16)
    inward = (
        col == ((row >> 1) & 7) * 32 + (row >> 7) * 16 + (row & 1) * 8 + ((row >> 4) & 7)
    ).astype(BF16)
    same = (row == col).astype(BF16)

    lane, sub = iota((8, 128), 1), iota((8, 128), 0)

    def build(step):
        half = (core + 1 + step) % 2

        def body(b, _):
            first = b // 2 * 32 + half * 16 + b % 2 * 8
            value = jnp.zeros((8, 128), jnp.int32)
            for u in range(8):
                value = jnp.where(sub == u, bins[first + u], value)
            c0, s0 = cos_sin((value * lane) & 2047)
            c1, s1 = cos_sin(((value * lane) & 15) * 128)
            rows = pl.ds(pl.multiple_of(b * 16, 16), 16)
            for u in range(16):
                ca = jnp.broadcast_to(c1[:, u:u + 1], (8, 128))
                sa = jnp.broadcast_to(s1[:, u:u + 1], (8, 128))
                both = jnp.concatenate([c0 * ca - s0 * sa, -(s0 * ca + c0 * sa)], axis=0)
                table[rows, u * 128:(u + 1) * 128] = both.astype(BF16)
            return 0

        lax.fori_loop(0, 16, body, 0)

    def transform(n):
        part = x_buf[pl.ds(pl.multiple_of(n * 256, 256), 256), :]
        spectrum = (dot_t(table[...], part) * (1.0 / math.sqrt(2048))).astype(BF16)
        for u in range(2):
            for b in range(16):
                tiles[pl.ds(pl.multiple_of(n * 32 + u * 16, 16), 16), b * 128:(b + 1) * 128] = (
                    spectrum[b * 16:(b + 1) * 16, u * 128:(u + 1) * 128]
                )

    def pack(step):
        def body(n, _):
            part = dot(outward, tiles[:, pl.ds(pl.multiple_of(n * 256, 256), 256)]).astype(BF16)
            for u in range(2):
                for j in range(8):
                    send[step * 128 + n * 16 + u * 8 + j] = part[j * 32:(j + 1) * 32, u * 128:(u + 1) * 128]
            return 0

        lax.fori_loop(0, 8, body, 0)

    mine = y * 64 + r * 8 + f

    def spread(step, k):
        to_x, to_y = (x + k // 2 % 4) % 4, (y + k // 8 % 4) % 4
        to_z = (z + k // 32 + k % 2 * 4) % 8
        place = step * 128 + (to_x * 2 + to_z // 4) * 16 + to_y * 4 + to_z % 4
        return place, device(to_x, to_y, to_z, (core + 1 + step) % 2)

    def push(step):
        def body(k, _):
            place, target = spread(step, k)
            pltpu.make_async_remote_copy(
                src_ref=send.at[place], dst_ref=received.at[mine], send_sem=send_sem.at[0],
                recv_sem=recv_sem.at[0], device_id=target, device_id_type=MESH,
            ).start()
            return 0

        lax.fori_loop(step, 128, body, 0)

    build(0)
    pl.semaphore_wait(barrier, 30)

    def confirm(k, _):
        pl.semaphore_signal(ready_sem, inc=1, device_id=along_xy(k), device_id_type=MESH)
        return 0

    lax.fori_loop(1, 16, confirm, 0)
    for n in range(8):
        load(n).wait()
        transform(n)
    pack(0)
    pl.semaphore_wait(ready_sem, 15)
    push(0)
    build(1)

    def body(n, _):
        transform(n)
        return 0

    lax.fori_loop(0, 8, body, 0)
    pack(1)
    place, _ = spread(1, 0)
    own = pltpu.make_async_copy(send.at[place], received.at[mine], own_sem.at[0])
    own.start()
    push(1)

    def picks(dim):
        slot = iota((512, 512), dim)
        wanted = slot & (PANEL - 1)
        for n in range(8):
            wanted = wanted + jnp.where(slot >> 6 == n, starts[n] * PANEL, 0)
        return (iota((512, 512), 1 - dim) == wanted).astype(BF16)

    chosen[0], chosen[1] = picks(0), picks(1)

    own.wait()
    all_but_one = received.at[pl.ds(0, 255)]
    pltpu.make_async_copy(all_but_one, all_but_one, recv_sem.at[0]).wait()

    def unpack(b, _):
        part = received[pl.ds(b * 16, 16)].reshape(512, 128)
        part = jnp.concatenate([part[:256], part[256:]], axis=1)
        part = dot(inward, part).astype(BF16)
        for u in range(2):
            for c in range(2):
                for i in range(8):
                    field[pl.ds(pl.multiple_of(c * 512 + b * 32 + u * 16, 16), 16), i * 128:(i + 1) * 128] = (
                        part[(c * 8 + i) * 16:(c * 8 + i + 1) * 16, u * 128:(u + 1) * 128]
                    )
        return 0

    lax.fori_loop(0, 16, unpack, 0)

    for h in range(2):
        rows = slice(h * 256, (h + 1) * 256)
        real = dot(field[rows, 0:512], chosen[1])
        imag = dot(field[512 + h * 256:512 + (h + 1) * 256, 0:512], chosen[1])
        left[rows, 0:512] = real.astype(BF16)
        left[rows, 512:1024] = (-imag).astype(BF16)
        rows = slice(512 + h * 256, 512 + (h + 1) * 256)
        left[rows, 0:512] = imag.astype(BF16)
        left[rows, 512:1024] = real.astype(BF16)

    entry = core * 16 + y * 4 + zl

    def multiply(t):
        to_zl = jnp.where(t == 0, (zl + 2) % 4, jnp.where(t == 1, 3 - zl, jnp.where(t == 2, zl + 1 - zl % 2 * 2, zl)))
        lanes = pl.ds(pl.multiple_of(to_zl * 256, 256), 256)
        right = jnp.concatenate(
            [dot(chosen[0], field[c * 512:(c + 1) * 512, lanes]).astype(BF16) for c in range(2)], axis=0
        )
        for c in range(2):
            sums = dot(left[c * 512:(c + 1) * 512, :], right) * (1.0 / math.sqrt(512))
            turned = dot_t(same, sums.astype(BF16)).astype(BF16)
            for to_core in range(2):
                for to_y in range(4):
                    blocks[t * 8 + to_core * 4 + to_y, c] = (
                        turned[to_core * 128:(to_core + 1) * 128, to_y * 128:(to_y + 1) * 128]
                    )
        return to_zl

    def deliver(t, to_zl, first):
        def body(k, _):
            to_core, to_y = (core + k % 2) % 2, (y + k // 2) % 4
            pltpu.make_async_remote_copy(
                src_ref=blocks.at[t * 8 + to_core * 4 + to_y], dst_ref=out.at[:, entry],
                send_sem=send_sem.at[1], recv_sem=recv_sem.at[1],
                device_id=(f, to_zl * 2 + to_core, to_y), device_id_type=MESH,
            ).start()
            return 0

        lax.fori_loop(first, 8, body, 0)

    def step(t, _):
        to_zl = multiply(t)
        deliver(t, to_zl, 0)
        return 0

    lax.fori_loop(0, 3, step, 0)
    multiply(3)
    last = pltpu.make_async_copy(blocks.at[24 + core * 4 + y], out.at[:, entry], own_sem.at[1])
    last.start()
    deliver(3, zl, 1)

    pltpu.make_async_copy(all_but_one, all_but_one, send_sem.at[0]).wait()
    last.wait()
    sent = blocks.at[pl.ds(0, 31)]
    pltpu.make_async_copy(sent, sent, recv_sem.at[1]).wait()
    pltpu.make_async_copy(sent, sent, send_sem.at[1]).wait()


def on_device(traces, band_bins, panel_start):
    return pl.pallas_call(
        kernel,
        out_shape=jax.ShapeDtypeStruct((2, 32, 128, 128), BF16),
        in_specs=[
            pl.BlockSpec(memory_space=pltpu.SMEM),
            pl.BlockSpec(memory_space=pltpu.SMEM),
            pl.BlockSpec(memory_space=pl.ANY),
        ],
        out_specs=pl.BlockSpec(memory_space=pltpu.VMEM),
        scratch_shapes=[
            pltpu.VMEM((2048, 2048), BF16),
            pltpu.VMEM((256, 2048), BF16),
            pltpu.VMEM((256, 2048), BF16),
            pltpu.VMEM((256, 32, 128), BF16),
            pltpu.VMEM((256, 32, 128), BF16),
            pltpu.VMEM((1024, 1024), BF16),
            pltpu.VMEM((1024, 1024), BF16),
            pltpu.VMEM((32, 2, 128, 128), BF16),
            pltpu.VMEM((2, 512, 512), BF16),
            pltpu.SemaphoreType.DMA((8,)),
            pltpu.SemaphoreType.DMA((2,)),
            pltpu.SemaphoreType.DMA((2,)),
            pltpu.SemaphoreType.DMA((2,)),
            pltpu.SemaphoreType.REGULAR,
        ],
        compiler_params=pltpu.CompilerParams(
            collective_id=0, has_side_effects=True, vmem_limit_bytes=48 * 2**20
        ),
        cost_estimate=pl.CostEstimate(flops=9_000_000_000, bytes_accessed=10 * 2**20, transcendentals=0),
        name="multiples",
    )(band_bins, panel_start, traces)


def solution(mesh):
    return jax.shard_map(
        on_device,
        mesh=mesh,
        in_specs=(P(("col", "row", "freq"), None, None), P(), P()),
        out_specs=P(None, "freq", "row", "col"),
        check_vma=False,
    )
```

```python
import functools
import math

import jax
import jax.numpy as jnp
from jax import lax
from jax.experimental import pallas as pl
from jax.experimental.pallas import tpu as pltpu
from jax.sharding import PartitionSpec as P

PANEL = 64
MESH = pl.DeviceIdType.MESH
BF16 = jnp.bfloat16
F32 = jnp.float32


def iota(shape, dim):
    return lax.broadcasted_iota(jnp.int32, shape, dim)


def dot(a, b):
    return lax.dot_general(a, b, (((1,), (0,)), ((), ())), preferred_element_type=F32)


def dot_t(a, b):
    return lax.dot_general(a, b, (((1,), (1,)), ((), ())), preferred_element_type=F32)


def cos_sin(phase):
    quadrant = ((phase + 256) >> 9) & 3
    rest = (phase - 512 * ((phase + 256) >> 9)).astype(F32) * (2.0 * math.pi / 2048)
    square = rest * rest
    sine = rest * (1.0 + square * (-1.0 / 6 + square * (1.0 / 120 + square * (-1.0 / 5040 + square * (1.0 / 362880)))))
    cosine = 1.0 + square * (-0.5 + square * (1.0 / 24 + square * (-1.0 / 720 + square * (1.0 / 40320 - square * (1.0 / 3628800)))))
    odd = (quadrant & 1) == 1
    first, second = jnp.where(odd, sine, cosine), jnp.where(odd, cosine, sine)
    first = jnp.where((quadrant == 1) | (quadrant == 2), -first, first)
    second = jnp.where(quadrant >= 2, -second, second)
    return first, second


def kernel(bins_in, starts_in, traces, out, bins, starts, x_buf, table, tiles, send, received, field, left, blocks,
           load_sem, small_sem, send_sem, recv_sem, own_sem, ready_sem):
    f, r, y = (lax.axis_index(n) for n in ("freq", "row", "col"))
    x, zh, zl, core = f // 2, f % 2, r // 2, r % 2
    z = zh * 4 + zl

    def device(x, y, z, core):
        return (x * 2 + z // 4, z % 4 * 2 + core, y)

    copy_bins = pltpu.make_async_copy(bins_in, bins, small_sem.at[0])
    copy_starts = pltpu.make_async_copy(starts_in, starts, small_sem.at[1])
    copy_bins.start()

    def load(n):
        return pltpu.make_async_copy(
            traces.at[n // 2, pl.ds(n % 2 * 512, 512)],
            x_buf.at[pl.ds(pl.multiple_of(n * 512, 512), 512)],
            load_sem.at[n],
        )

    for n in range(4):
        load(n).start()
    copy_starts.start()

    barrier = pltpu.get_barrier_semaphore()

    def along_z(k):
        return device(x, y, (z + k // 2) % 8, (core + k % 2) % 2)

    def along_xy(k):
        return device((x + k // 4) % 4, (y + k % 4) % 4, z, core)

    def greet(k, _):
        pl.semaphore_signal(barrier, inc=1, device_id=along_z(k), device_id_type=MESH)
        pl.semaphore_signal(barrier, inc=1, device_id=along_xy(k), device_id_type=MESH)
        return 0

    lax.fori_loop(1, 16, greet, 0)

    row, col = iota((256, 256), 0), iota((256, 256), 1)
    outward = (col == (row & 15) * 16 + ((row >> 4) & 1) * 8 + (row >> 5)).astype(BF16)
    inward = (
        col == ((row >> 1) & 7) * 32 + (row >> 7) * 16 + (row & 1) * 8 + ((row >> 4) & 7)
    ).astype(BF16)

    lane, sub = iota((8, 128), 1), iota((8, 128), 0)

    def build(step):
        half = (core + 1 + step) % 2

        def body(b, _):
            first = b // 2 * 32 + half * 16 + b % 2 * 8
            value = jnp.zeros((8, 128), jnp.int32)
            for u in range(8):
                value = jnp.where(sub == u, bins[first + u], value)
            c0, s0 = cos_sin((value * lane) & 2047)
            c1, s1 = cos_sin(((value * lane) & 15) * 128)
            rows = pl.ds(pl.multiple_of(b * 16, 16), 16)
            for u in range(16):
                ca = jnp.broadcast_to(c1[:, u:u + 1], (8, 128))
                sa = jnp.broadcast_to(s1[:, u:u + 1], (8, 128))
                both = jnp.concatenate([c0 * ca - s0 * sa, -(s0 * ca + c0 * sa)], axis=0)
                table[rows, u * 128:(u + 1) * 128] = both.astype(BF16)
            return 0

        lax.fori_loop(0, 16, body, 0, unroll=2)

    def transform(step):
        def body(n, _):
            if step == 0:
                load(n).wait()
            part = x_buf[pl.ds(pl.multiple_of(n * 512, 512), 512), :]
            spectrum = (dot_t(table[...], part) * (1.0 / math.sqrt(2048))).astype(BF16)
            for u in range(4):
                for b in range(16):
                    tiles[pl.ds(pl.multiple_of(n * 64 + u * 16, 16), 16), b * 128:(b + 1) * 128] = (
                        spectrum[b * 16:(b + 1) * 16, u * 128:(u + 1) * 128]
                    )
            return 0

        lax.fori_loop(0, 4, body, 0)

    def pack(step):
        for n in range(8):
            part = dot(outward, tiles[:, n * 256:(n + 1) * 256]).astype(BF16)
            for u in range(2):
                for j in range(8):
                    send[step * 128 + n * 16 + u * 8 + j] = part[j * 32:(j + 1) * 32, u * 128:(u + 1) * 128]

    mine = y * 64 + r * 8 + f

    def spread(step, k):
        to_x, to_y = (x + k // 2 % 4) % 4, (y + k // 8 % 4) % 4
        to_z = (z + k // 32 + k % 2 * 4) % 8
        place = step * 128 + (to_x * 2 + to_z // 4) * 16 + to_y * 4 + to_z % 4
        return place, device(to_x, to_y, to_z, (core + 1 + step) % 2)

    def push(step):
        def body(k, _):
            place, target = spread(step, k)
            pltpu.make_async_remote_copy(
                src_ref=send.at[place], dst_ref=received.at[mine], send_sem=send_sem.at[0],
                recv_sem=recv_sem.at[step * 4 + k // 32], device_id=target, device_id_type=MESH,
            ).start()
            return 0

        lax.fori_loop(step, 128, body, 0)

    copy_bins.wait()
    build(0)
    pl.semaphore_wait(barrier, 30)

    def confirm(k, _):
        pl.semaphore_signal(ready_sem, inc=1, device_id=along_xy(k), device_id_type=MESH)
        return 0

    lax.fori_loop(1, 16, confirm, 0)
    transform(0)
    pack(0)
    pl.semaphore_wait(ready_sem, 15)
    push(0)
    build(1)
    transform(1)
    pack(1)
    place, _ = spread(1, 0)
    own = pltpu.make_async_copy(send.at[place], received.at[mine], own_sem.at[0])
    own.start()
    push(1)

    copy_starts.wait()
    lane = iota((16, 512), 1)
    weight = jnp.zeros((16, 512), F32)
    for n in range(8):
        weight = weight + jnp.where(lane >> 6 == starts[n], 1.0, 0.0)

    def unpack(g):
        block = (zl + 4 - g % 4) % 4 * 2 + (core + 1 + g // 4) % 2
        if g == 4:
            own.wait()
        arrived = received.at[pl.ds(0, 31 if g == 4 else 32)]
        pltpu.make_async_copy(arrived, arrived, recv_sem.at[g]).wait()
        for v in range(2):
            part = jnp.concatenate(
                [received[pl.ds((v * 2 + u) * 64 + block * 8, 8)].reshape(256, 128) for u in range(2)], axis=1
            )
            part = dot(inward, part)
            for u in range(2):
                first = (v * 2 + u) * 128 + block * 16
                upper, lower = pl.ds(pl.multiple_of(first, 16), 16), pl.ds(pl.multiple_of(512 + first, 16), 16)
                for c in range(2):
                    for i in range(8):
                        value = part[(c * 8 + i) * 16:(c * 8 + i + 1) * 16, u * 128:(u + 1) * 128]
                        field[lower if c else upper, i * 128:(i + 1) * 128] = value.astype(BF16)
                        if i < 4:
                            value = value * weight[:, i * 128:(i + 1) * 128]
                            one, two = slice(i * 128, (i + 1) * 128), slice(512 + i * 128, 512 + (i + 1) * 128)
                            if c == 0:
                                left[upper, one] = value.astype(BF16)
                                left[lower, two] = value.astype(BF16)
                            else:
                                left[lower, one] = value.astype(BF16)
                                left[upper, two] = (-value).astype(BF16)

    for g in range(8):
        unpack(g)

    entry = core * 16 + y * 4 + zl

    def multiply(t, first):
        to_zl = jnp.where(t == 0, (zl + 2) % 4, jnp.where(t == 1, 3 - zl, jnp.where(t == 2, zl + 1 - zl % 2 * 2, zl)))
        lanes = pl.ds(pl.multiple_of(to_zl * 256, 256), 256)
        for c in range(2):
            sums = dot(left[c * 512:(c + 1) * 512, :], field[:, lanes]) * (1.0 / math.sqrt(512))
            turned = sums.astype(BF16).T
            for to_core in range(2):
                for to_y in range(4):
                    blocks[t * 16 + c * 8 + to_core * 4 + to_y] = (
                        turned[to_core * 128:(to_core + 1) * 128, to_y * 128:(to_y + 1) * 128]
                    )

            def body(k, _):
                to_core, to_y = (core + k % 2) % 2, (y + k // 2) % 4
                pltpu.make_async_remote_copy(
                    src_ref=blocks.at[t * 16 + c * 8 + to_core * 4 + to_y], dst_ref=out.at[c, entry],
                    send_sem=send_sem.at[1], recv_sem=recv_sem.at[8],
                    device_id=(f, to_zl * 2 + to_core, to_y), device_id_type=MESH,
                ).start()
                return 0

            lax.fori_loop(first, 8, body, 0)

    def step(t, _):
        multiply(t, 0)
        return 0

    lax.fori_loop(0, 3, step, 0)
    multiply(3, 1)
    last = [
        pltpu.make_async_copy(blocks.at[48 + c * 8 + core * 4 + y], out.at[c, entry], own_sem.at[1 + c])
        for c in range(2)
    ]
    for c in range(2):
        last[c].start()

    sent = send.at[pl.ds(0, 255)]
    pltpu.make_async_copy(sent, sent, send_sem.at[0]).wait()
    for c in range(2):
        last[c].wait()
    sent = blocks.at[pl.ds(0, 62)]
    pltpu.make_async_copy(sent, sent, recv_sem.at[8]).wait()
    pltpu.make_async_copy(sent, sent, send_sem.at[1]).wait()


def on_device(traces, band_bins, panel_start):
    return pl.pallas_call(
        kernel,
        out_shape=jax.ShapeDtypeStruct((2, 32, 128, 128), BF16),
        in_specs=[
            pl.BlockSpec(memory_space=pl.ANY),
            pl.BlockSpec(memory_space=pl.ANY),
            pl.BlockSpec(memory_space=pl.ANY),
        ],
        out_specs=pl.BlockSpec(memory_space=pltpu.VMEM),
        scratch_shapes=[
            pltpu.SMEM((256,), jnp.int32),
            pltpu.SMEM((8,), jnp.int32),
            pltpu.VMEM((2048, 2048), BF16),
            pltpu.VMEM((256, 2048), BF16),
            pltpu.VMEM((256, 2048), BF16),
            pltpu.VMEM((256, 32, 128), BF16),
            pltpu.VMEM((256, 32, 128), BF16),
            pltpu.VMEM((1024, 1024), BF16),
            pltpu.VMEM((1024, 1024), BF16),
            pltpu.VMEM((64, 128, 128), BF16),
            pltpu.SemaphoreType.DMA((4,)),
            pltpu.SemaphoreType.DMA((2,)),
            pltpu.SemaphoreType.DMA((2,)),
            pltpu.SemaphoreType.DMA((9,)),
            pltpu.SemaphoreType.DMA((3,)),
            pltpu.SemaphoreType.REGULAR,
        ],
        compiler_params=pltpu.CompilerParams(
            collective_id=0, has_side_effects=True, vmem_limit_bytes=48 * 2**20
        ),
        cost_estimate=pl.CostEstimate(flops=9_000_000_000, bytes_accessed=10 * 2**20, transcendentals=0),
        name="multiples",
    )(band_bins, panel_start, traces)


def solution(mesh):
    return jax.shard_map(
        on_device,
        mesh=mesh,
        in_specs=(P(("col", "row", "freq"), None, None), P(), P()),
        out_specs=P(None, "freq", "row", "col"),
        check_vma=False,
    )
```

```python
import functools
import math

import jax
import jax.numpy as jnp
from jax import lax
from jax.experimental import pallas as pl
from jax.experimental.pallas import tpu as pltpu
from jax.sharding import PartitionSpec as P

PANEL = 64
MESH = pl.DeviceIdType.MESH
BF16 = jnp.bfloat16
F32 = jnp.float32


def iota(shape, dim):
    return lax.broadcasted_iota(jnp.int32, shape, dim)


def dot(a, b):
    return lax.dot_general(a, b, (((1,), (0,)), ((), ())), preferred_element_type=F32)


def dot_t(a, b):
    return lax.dot_general(a, b, (((1,), (1,)), ((), ())), preferred_element_type=F32)


def cos_sin(phase):
    quadrant = ((phase + 256) >> 9) & 3
    rest = (phase - 512 * ((phase + 256) >> 9)).astype(F32) * (2.0 * math.pi / 2048)
    square = rest * rest
    sine = rest * (1.0 + square * (-1.0 / 6 + square * (1.0 / 120 + square * (-1.0 / 5040 + square * (1.0 / 362880)))))
    cosine = 1.0 + square * (-0.5 + square * (1.0 / 24 + square * (-1.0 / 720 + square * (1.0 / 40320 - square * (1.0 / 3628800)))))
    odd = (quadrant & 1) == 1
    first, second = jnp.where(odd, sine, cosine), jnp.where(odd, cosine, sine)
    first = jnp.where((quadrant == 1) | (quadrant == 2), -first, first)
    second = jnp.where(quadrant >= 2, -second, second)
    return first, second


def kernel(bins_in, starts_in, traces, out, bins, starts, x_buf, table, tiles, send, received, field, left, blocks,
           load_sem, small_sem, send_sem, recv_sem, own_sem, ready_sem):
    f, r, y = (lax.axis_index(n) for n in ("freq", "row", "col"))
    x, zh, zl, core = f // 2, f % 2, r // 2, r % 2
    z = zh * 4 + zl

    def device(x, y, z, core):
        return (x * 2 + z // 4, z % 4 * 2 + core, y)

    copy_bins = pltpu.make_async_copy(bins_in, bins, small_sem.at[0])
    copy_starts = pltpu.make_async_copy(starts_in, starts, small_sem.at[1])
    copy_bins.start()

    def load(n):
        return pltpu.make_async_copy(
            traces.at[n // 2, pl.ds(n % 2 * 512, 512)],
            x_buf.at[pl.ds(pl.multiple_of(n * 512, 512), 512)],
            load_sem.at[n],
        )

    for n in range(4):
        load(n).start()
    copy_starts.start()

    barrier = pltpu.get_barrier_semaphore()

    def along_z(k):
        return device(x, y, (z + k // 2) % 8, (core + k % 2) % 2)

    def along_xy(k):
        return device((x + k // 4) % 4, (y + k % 4) % 4, z, core)

    def greet(k, _):
        pl.semaphore_signal(barrier, inc=1, device_id=along_z(k), device_id_type=MESH)
        pl.semaphore_signal(barrier, inc=1, device_id=along_xy(k), device_id_type=MESH)
        return 0

    lax.fori_loop(1, 16, greet, 0)

    row, col = iota((256, 256), 0), iota((256, 256), 1)
    outward = (col == (row & 15) * 16 + ((row >> 4) & 1) * 8 + (row >> 5)).astype(BF16)
    inward = (
        col == ((row >> 1) & 7) * 32 + (row >> 7) * 16 + (row & 1) * 8 + ((row >> 4) & 7)
    ).astype(BF16)

    lane, sub = iota((8, 128), 1), iota((8, 128), 0)

    def build(q):
        half = (core + 1 + q // 2) % 2

        def body(b, _):
            value = jnp.zeros((8, 128), jnp.int32)
            for u in range(8):
                to_y = (y + q % 2 * 2 + u // 4) % 4
                value = jnp.where(sub == u, bins[b * 32 + half * 16 + to_y * 4 + u % 4], value)
            c0, s0 = cos_sin((value * lane) & 2047)
            c1, s1 = cos_sin(((value * lane) & 15) * 128)
            rows = pl.ds(pl.multiple_of(b * 16, 16), 16)
            for u in range(16):
                ca = jnp.broadcast_to(c1[:, u:u + 1], (8, 128))
                sa = jnp.broadcast_to(s1[:, u:u + 1], (8, 128))
                both = jnp.concatenate([c0 * ca - s0 * sa, -(s0 * ca + c0 * sa)], axis=0)
                table[rows, u * 128:(u + 1) * 128] = both.astype(BF16)
            return 0

        lax.fori_loop(0, 8, body, 0, unroll=2)

    def transform(n):
        part = x_buf[pl.ds(pl.multiple_of(n * 512, 512), 512), :]
        spectrum = (dot_t(table[...], part) * (1.0 / math.sqrt(2048))).astype(BF16)
        for u in range(4):
            for b in range(8):
                tiles[pl.ds(pl.multiple_of(n * 64 + u * 16, 16), 16), b * 128:(b + 1) * 128] = (
                    spectrum[b * 16:(b + 1) * 16, u * 128:(u + 1) * 128]
                )

    def pack(q):
        for n in range(4):
            part = dot(outward, tiles[:, n * 256:(n + 1) * 256]).astype(BF16)
            for u in range(2):
                for j in range(8):
                    send[q * 64 + n * 16 + u * 8 + j] = part[j * 32:(j + 1) * 32, u * 128:(u + 1) * 128]

    mine = y * 64 + r * 8 + f

    def spread(q, k):
        to_x, to_y = (x + (k // 8 % 4)) % 4, (y + q % 2 * 2 + (k // 32 % 2)) % 4
        to_z = (z + (k // 1 % 4) + (k // 4 % 2) * 4) % 8
        place = q * 64 + (to_x * 2 + to_z // 4) * 8 + (k // 32 % 2) * 4 + to_z % 4
        return place, device(to_x, to_y, to_z, (core + 1 + q // 2) % 2)

    def push(q):
        def body(k, _):
            place, target = spread(q, k)
            pltpu.make_async_remote_copy(
                src_ref=send.at[place], dst_ref=received.at[mine], send_sem=send_sem.at[0],
                recv_sem=recv_sem.at[q * 4 + (k // 1 % 4)], device_id=target, device_id_type=MESH,
            ).start()
            return 0

        lax.fori_loop(jnp.where(q == 2, 1, 0), 64, body, 0)

    copy_bins.wait()
    build(0)
    for n in range(2):
        load(n).wait()
        transform(n)
    pl.semaphore_wait(barrier, 30)

    def confirm(k, _):
        pl.semaphore_signal(ready_sem, inc=1, device_id=along_xy(k), device_id_type=MESH)
        return 0

    lax.fori_loop(1, 16, confirm, 0)
    for n in range(2, 4):
        load(n).wait()
        transform(n)
    pack(0)
    pl.semaphore_wait(ready_sem, 15)
    push(0)

    def quarter(q, _):
        def body(n, _):
            transform(n)
            return 0

        build(q)
        lax.fori_loop(0, 4, body, 0)
        pack(q)
        push(q)
        return 0

    lax.fori_loop(1, 4, quarter, 0)
    place, _ = spread(2, 0)
    own = pltpu.make_async_copy(send.at[place], received.at[mine], own_sem.at[0])
    own.start()

    copy_starts.wait()
    lane = iota((16, 512), 1)
    weight = jnp.zeros((16, 512), F32)
    for n in range(8):
        weight = weight + jnp.where(lane >> 6 == starts[n], 1.0, 0.0)

    def unpack(g):
        q = g // 4
        from_r = (zl + 4 - g % 4) % 4 * 2 + (core + 1 + q // 2) % 2
        block = [(y + 8 - q % 2 * 2 - u) % 4 * 8 + from_r for u in range(2)]
        if g == 8:
            own.wait()
        arrived = received.at[pl.ds(0, 15 if g == 8 else 16)]
        pltpu.make_async_copy(arrived, arrived, recv_sem.at[g]).wait()
        part = jnp.concatenate(
            [received[pl.ds(block[u] * 8, 8)].reshape(256, 128) for u in range(2)], axis=1
        )
        part = dot(inward, part)
        for u in range(2):
            first = block[u] * 16
            upper, lower = pl.ds(pl.multiple_of(first, 16), 16), pl.ds(pl.multiple_of(512 + first, 16), 16)
            for c in range(2):
                for i in range(8):
                    value = part[(c * 8 + i) * 16:(c * 8 + i + 1) * 16, u * 128:(u + 1) * 128]
                    field[lower if c else upper, i * 128:(i + 1) * 128] = value.astype(BF16)
                    if i < 4:
                        value = value * weight[:, i * 128:(i + 1) * 128]
                        one, two = slice(i * 128, (i + 1) * 128), slice(512 + i * 128, 512 + (i + 1) * 128)
                        if c == 0:
                            left[upper, one] = value.astype(BF16)
                            left[lower, two] = value.astype(BF16)
                        else:
                            left[lower, one] = value.astype(BF16)
                            left[upper, two] = (-value).astype(BF16)

    for g in range(16):
        unpack(g)

    entry = core * 16 + y * 4 + zl

    def multiply(t, first):
        to_zl = jnp.where(t == 0, (zl + 2) % 4, jnp.where(t == 1, 3 - zl, jnp.where(t == 2, zl + 1 - zl % 2 * 2, zl)))
        lanes = pl.ds(pl.multiple_of(to_zl * 256, 256), 256)
        for c in range(2):
            sums = dot(left[c * 512:(c + 1) * 512, :], field[:, lanes]) * (1.0 / math.sqrt(512))
            turned = sums.astype(BF16).T
            for to_core in range(2):
                for to_y in range(4):
                    blocks[t * 16 + c * 8 + to_core * 4 + to_y] = (
                        turned[to_core * 128:(to_core + 1) * 128, to_y * 128:(to_y + 1) * 128]
                    )

            def body(k, _):
                to_core, to_y = (core + k % 2) % 2, (y + k // 2) % 4
                pltpu.make_async_remote_copy(
                    src_ref=blocks.at[t * 16 + c * 8 + to_core * 4 + to_y], dst_ref=out.at[c, entry],
                    send_sem=send_sem.at[1], recv_sem=recv_sem.at[16],
                    device_id=(f, to_zl * 2 + to_core, to_y), device_id_type=MESH,
                ).start()
                return 0

            lax.fori_loop(first, 8, body, 0)

    def step(t, _):
        multiply(t, 0)
        return 0

    lax.fori_loop(0, 3, step, 0)
    multiply(3, 1)
    last = [
        pltpu.make_async_copy(blocks.at[48 + c * 8 + core * 4 + y], out.at[c, entry], own_sem.at[1 + c])
        for c in range(2)
    ]
    for c in range(2):
        last[c].start()

    sent = send.at[pl.ds(0, 255)]
    pltpu.make_async_copy(sent, sent, send_sem.at[0]).wait()
    for c in range(2):
        last[c].wait()
    sent = blocks.at[pl.ds(0, 62)]
    pltpu.make_async_copy(sent, sent, recv_sem.at[16]).wait()
    pltpu.make_async_copy(sent, sent, send_sem.at[1]).wait()


def on_device(traces, band_bins, panel_start):
    return pl.pallas_call(
        kernel,
        out_shape=jax.ShapeDtypeStruct((2, 32, 128, 128), BF16),
        in_specs=[
            pl.BlockSpec(memory_space=pl.ANY),
            pl.BlockSpec(memory_space=pl.ANY),
            pl.BlockSpec(memory_space=pl.ANY),
        ],
        out_specs=pl.BlockSpec(memory_space=pltpu.VMEM),
        scratch_shapes=[
            pltpu.SMEM((256,), jnp.int32),
            pltpu.SMEM((8,), jnp.int32),
            pltpu.VMEM((2048, 2048), BF16),
            pltpu.VMEM((128, 2048), BF16),
            pltpu.VMEM((256, 1024), BF16),
            pltpu.VMEM((256, 32, 128), BF16),
            pltpu.VMEM((256, 32, 128), BF16),
            pltpu.VMEM((1024, 1024), BF16),
            pltpu.VMEM((1024, 1024), BF16),
            pltpu.VMEM((64, 128, 128), BF16),
            pltpu.SemaphoreType.DMA((4,)),
            pltpu.SemaphoreType.DMA((2,)),
            pltpu.SemaphoreType.DMA((2,)),
            pltpu.SemaphoreType.DMA((17,)),
            pltpu.SemaphoreType.DMA((3,)),
            pltpu.SemaphoreType.REGULAR,
        ],
        compiler_params=pltpu.CompilerParams(
            collective_id=0, has_side_effects=True, vmem_limit_bytes=48 * 2**20
        ),
        cost_estimate=pl.CostEstimate(flops=9_000_000_000, bytes_accessed=10 * 2**20, transcendentals=0),
        name="multiples",
    )(*(pltpu.with_memory_space_constraint(v, pltpu.HBM) for v in (band_bins, panel_start, traces)))


def solution(mesh):
    return jax.shard_map(
        on_device,
        mesh=mesh,
        in_specs=(P(("col", "row", "freq"), None, None), P(), P()),
        out_specs=P(None, "freq", "row", "col"),
        check_vma=False,
    )
```

```python
import functools
import math

import jax
import jax.numpy as jnp
from jax import lax
from jax.experimental import pallas as pl
from jax.experimental.pallas import tpu as pltpu
from jax.sharding import PartitionSpec as P

PANEL = 64
MESH = pl.DeviceIdType.MESH
BF16 = jnp.bfloat16
F32 = jnp.float32


def iota(shape, dim):
    return lax.broadcasted_iota(jnp.int32, shape, dim)


def dot(a, b):
    return lax.dot_general(a, b, (((1,), (0,)), ((), ())), preferred_element_type=F32)


def dot_t(a, b):
    return lax.dot_general(a, b, (((1,), (1,)), ((), ())), preferred_element_type=F32)


def cos_sin(phase):
    quadrant = ((phase + 256) >> 9) & 3
    rest = (phase - 512 * ((phase + 256) >> 9)).astype(F32) * (2.0 * math.pi / 2048)
    square = rest * rest
    sine = rest * (1.0 + square * (-1.0 / 6 + square * (1.0 / 120 + square * (-1.0 / 5040 + square * (1.0 / 362880)))))
    cosine = 1.0 + square * (-0.5 + square * (1.0 / 24 + square * (-1.0 / 720 + square * (1.0 / 40320 - square * (1.0 / 3628800)))))
    odd = (quadrant & 1) == 1
    first, second = jnp.where(odd, sine, cosine), jnp.where(odd, cosine, sine)
    first = jnp.where((quadrant == 1) | (quadrant == 2), -first, first)
    second = jnp.where(quadrant >= 2, -second, second)
    return first, second


def kernel(bins_in, starts_in, traces, out, bins, starts, x_buf, table, tiles, send, received, field, left, blocks,
           load_sem, small_sem, send_sem, recv_sem, own_sem, ready_sem):
    f, r, y = (lax.axis_index(n) for n in ("freq", "row", "col"))
    x, zh, zl, core = f // 2, f % 2, r // 2, r % 2
    z = zh * 4 + zl

    def device(x, y, z, core):
        return (x * 2 + z // 4, z % 4 * 2 + core, y)

    barrier = pltpu.get_barrier_semaphore()

    def along_z(k):
        return device(x, y, (z + k // 2) % 8, (core + k % 2) % 2)

    def along_xy(k):
        return device((x + k // 4) % 4, (y + k % 4) % 4, z, core)

    for k in range(1, 16):
        pl.semaphore_signal(barrier, inc=1, device_id=along_z(k), device_id_type=MESH)
    for k in range(1, 16):
        pl.semaphore_signal(barrier, inc=1, device_id=along_xy(k), device_id_type=MESH)

    copy_bins = pltpu.make_async_copy(bins_in, bins, small_sem.at[0])
    copy_starts = pltpu.make_async_copy(starts_in, starts, small_sem.at[1])
    copy_bins.start()

    def load(n):
        return pltpu.make_async_copy(
            traces.at[n // 2, pl.ds(n % 2 * 512, 512)],
            x_buf.at[pl.ds(pl.multiple_of(n * 512, 512), 512)],
            load_sem.at[n],
        )

    for n in range(4):
        load(n).start()
    copy_starts.start()

    row, col = iota((256, 256), 0), iota((256, 256), 1)
    outward = (col == (row & 15) * 16 + ((row >> 4) & 1) * 8 + (row >> 5)).astype(BF16)
    inward = (
        col == ((row >> 1) & 7) * 32 + (row >> 7) * 16 + (row & 1) * 8 + ((row >> 4) & 7)
    ).astype(BF16)

    lane, sub = iota((8, 128), 1), iota((8, 128), 0)

    def build(q):
        half = (core + 1 + q // 2) % 2

        def body(b, _):
            value = jnp.zeros((8, 128), jnp.int32)
            for u in range(8):
                to_y = (y + q % 2 * 2 + u // 4) % 4
                value = jnp.where(sub == u, bins[b * 32 + half * 16 + to_y * 4 + u % 4], value)
            c0, s0 = cos_sin((value * lane) & 2047)
            c1, s1 = cos_sin(((value * lane) & 15) * 128)
            rows = pl.ds(pl.multiple_of(b * 16, 16), 16)
            for u in range(16):
                ca = jnp.broadcast_to(c1[:, u:u + 1], (8, 128))
                sa = jnp.broadcast_to(s1[:, u:u + 1], (8, 128))
                both = jnp.concatenate([c0 * ca - s0 * sa, -(s0 * ca + c0 * sa)], axis=0)
                table[rows, u * 128:(u + 1) * 128] = both.astype(BF16)
            return 0

        lax.fori_loop(0, 8, body, 0, unroll=2)

    def transform(n):
        part = x_buf[pl.ds(pl.multiple_of(n * 512, 512), 512), :]
        spectrum = (dot_t(table[...], part) * (1.0 / math.sqrt(2048))).astype(BF16)
        for u in range(4):
            for b in range(8):
                tiles[pl.ds(pl.multiple_of(n * 64 + u * 16, 16), 16), b * 128:(b + 1) * 128] = (
                    spectrum[b * 16:(b + 1) * 16, u * 128:(u + 1) * 128]
                )

    def pack(q):
        for n in range(4):
            part = dot(outward, tiles[:, n * 256:(n + 1) * 256]).astype(BF16)
            for u in range(2):
                for j in range(8):
                    send[q * 64 + n * 16 + u * 8 + j] = part[j * 32:(j + 1) * 32, u * 128:(u + 1) * 128]

    mine = y * 64 + r * 8 + f

    def spread(q, k):
        to_x, to_y = (x + (k // 8 % 4)) % 4, (y + q % 2 * 2 + (k // 32 % 2)) % 4
        to_z = (z + (k // 1 % 4) + (k // 4 % 2) * 4) % 8
        place = q * 64 + (to_x * 2 + to_z // 4) * 8 + (k // 32 % 2) * 4 + to_z % 4
        return place, device(to_x, to_y, to_z, (core + 1 + q // 2) % 2)

    def push(q):
        def body(k, _):
            place, target = spread(q, k)
            pltpu.make_async_remote_copy(
                src_ref=send.at[place], dst_ref=received.at[mine], send_sem=send_sem.at[0],
                recv_sem=recv_sem.at[q * 4 + (k // 1 % 4)], device_id=target, device_id_type=MESH,
            ).start()
            return 0

        lax.fori_loop(jnp.where(q == 2, 1, 0), 64, body, 0)

    copy_bins.wait()
    build(0)
    for n in range(1):
        load(n).wait()
        transform(n)
    pl.semaphore_wait(barrier, 30)

    for k in range(1, 16):
        pl.semaphore_signal(ready_sem, inc=1, device_id=along_xy(k), device_id_type=MESH)
    for n in range(1, 4):
        load(n).wait()
        transform(n)
    pack(0)
    pl.semaphore_wait(ready_sem, 15)
    push(0)

    def quarter(q, _):
        def body(n, _):
            transform(n)
            return 0

        build(q)
        lax.fori_loop(0, 4, body, 0)
        pack(q)
        push(q)
        return 0

    lax.fori_loop(1, 4, quarter, 0)
    place, _ = spread(2, 0)
    own = pltpu.make_async_copy(send.at[place], received.at[mine], own_sem.at[0])
    own.start()

    copy_starts.wait()
    lane = iota((16, 512), 1)
    weight = jnp.zeros((16, 512), F32)
    for n in range(8):
        weight = weight + jnp.where(lane >> 6 == starts[n], 1.0, 0.0)

    def unpack(g):
        q = g // 4
        from_r = (zl + 4 - g % 4) % 4 * 2 + (core + 1 + q // 2) % 2
        block = [(y + 8 - q % 2 * 2 - u) % 4 * 8 + from_r for u in range(2)]
        if g == 8:
            own.wait()
        arrived = received.at[pl.ds(0, 15 if g == 8 else 16)]
        pltpu.make_async_copy(arrived, arrived, recv_sem.at[g]).wait()
        part = jnp.concatenate(
            [received[pl.ds(block[u] * 8, 8)].reshape(256, 128) for u in range(2)], axis=1
        )
        part = dot(inward, part)
        for u in range(2):
            first = block[u] * 16
            upper, lower = pl.ds(pl.multiple_of(first, 16), 16), pl.ds(pl.multiple_of(512 + first, 16), 16)
            for c in range(2):
                for i in range(8):
                    value = part[(c * 8 + i) * 16:(c * 8 + i + 1) * 16, u * 128:(u + 1) * 128]
                    field[lower if c else upper, i * 128:(i + 1) * 128] = value.astype(BF16)
                    if i < 4:
                        value = value * weight[:, i * 128:(i + 1) * 128]
                        one, two = slice(i * 128, (i + 1) * 128), slice(512 + i * 128, 512 + (i + 1) * 128)
                        if c == 0:
                            left[upper, one] = value.astype(BF16)
                            left[lower, two] = value.astype(BF16)
                        else:
                            left[lower, one] = value.astype(BF16)
                            left[upper, two] = (-value).astype(BF16)

    for g in range(16):
        unpack(g)

    entry = core * 16 + y * 4 + zl

    def multiply(t):
        to_zl = jnp.where(t == 0, (zl + 2) % 4, jnp.where(t == 1, 3 - zl, jnp.where(t == 2, zl + 1 - zl % 2 * 2, zl)))
        lanes = pl.ds(pl.multiple_of(to_zl * 256, 256), 256)
        for part in range(4):
            c, pair = part // 2, part % 2
            rows = slice(part * 256, (part + 1) * 256)
            sums = dot(left[rows, :], field[:, lanes]) * (1.0 / math.sqrt(512))
            turned = sums.astype(BF16).T
            for to_core in range(2):
                for u in range(2):
                    blocks[t * 16 + c * 8 + to_core * 4 + pair * 2 + u] = (
                        turned[to_core * 128:(to_core + 1) * 128, u * 128:(u + 1) * 128]
                    )

            def body(k, _):
                to_core, to_y = k % 2, pair * 2 + k // 2

                @pl.when((t < 3) | (to_core != core) | (to_y != y))
                def _():
                    pltpu.make_async_remote_copy(
                        src_ref=blocks.at[t * 16 + c * 8 + to_core * 4 + to_y], dst_ref=out.at[c, entry],
                        send_sem=send_sem.at[1], recv_sem=recv_sem.at[16],
                        device_id=(f, to_zl * 2 + to_core, to_y), device_id_type=MESH,
                    ).start()

                return 0

            lax.fori_loop(0, 4, body, 0)

    def step(t, _):
        multiply(t)
        return 0

    lax.fori_loop(0, 3, step, 0)
    multiply(3)
    last = [
        pltpu.make_async_copy(blocks.at[48 + c * 8 + core * 4 + y], out.at[c, entry], own_sem.at[1 + c])
        for c in range(2)
    ]
    for c in range(2):
        last[c].start()

    sent = send.at[pl.ds(0, 255)]
    pltpu.make_async_copy(sent, sent, send_sem.at[0]).wait()
    for c in range(2):
        last[c].wait()
    sent = blocks.at[pl.ds(0, 62)]
    pltpu.make_async_copy(sent, sent, recv_sem.at[16]).wait()
    pltpu.make_async_copy(sent, sent, send_sem.at[1]).wait()


def on_device(traces, band_bins, panel_start):
    return pl.pallas_call(
        kernel,
        out_shape=jax.ShapeDtypeStruct((2, 32, 128, 128), BF16),
        in_specs=[
            pl.BlockSpec(memory_space=pl.ANY),
            pl.BlockSpec(memory_space=pl.ANY),
            pl.BlockSpec(memory_space=pl.ANY),
        ],
        out_specs=pl.BlockSpec(memory_space=pltpu.VMEM),
        scratch_shapes=[
            pltpu.SMEM((256,), jnp.int32),
            pltpu.SMEM((8,), jnp.int32),
            pltpu.VMEM((2048, 2048), BF16),
            pltpu.VMEM((128, 2048), BF16),
            pltpu.VMEM((256, 1024), BF16),
            pltpu.VMEM((256, 32, 128), BF16),
            pltpu.VMEM((256, 32, 128), BF16),
            pltpu.VMEM((1024, 1024), BF16),
            pltpu.VMEM((1024, 1024), BF16),
            pltpu.VMEM((64, 128, 128), BF16),
            pltpu.SemaphoreType.DMA((4,)),
            pltpu.SemaphoreType.DMA((2,)),
            pltpu.SemaphoreType.DMA((2,)),
            pltpu.SemaphoreType.DMA((17,)),
            pltpu.SemaphoreType.DMA((3,)),
            pltpu.SemaphoreType.REGULAR,
        ],
        compiler_params=pltpu.CompilerParams(
            collective_id=0, has_side_effects=True, vmem_limit_bytes=48 * 2**20
        ),
        cost_estimate=pl.CostEstimate(flops=9_000_000_000, bytes_accessed=10 * 2**20, transcendentals=0),
        name="multiples",
    )(*(pltpu.with_memory_space_constraint(v, pltpu.HBM) for v in (band_bins, panel_start, traces)))


def solution(mesh):
    return jax.shard_map(
        on_device,
        mesh=mesh,
        in_specs=(P(("col", "row", "freq"), None, None), P(), P()),
        out_specs=P(None, "freq", "row", "col"),
        check_vma=False,
    )
```

```python
import functools
import math

import jax
import jax.numpy as jnp
from jax import lax
from jax.experimental import pallas as pl
from jax.experimental.pallas import tpu as pltpu
from jax.sharding import PartitionSpec as P

PANEL = 64
MESH = pl.DeviceIdType.MESH
BF16 = jnp.bfloat16
F32 = jnp.float32


def iota(shape, dim):
    return lax.broadcasted_iota(jnp.int32, shape, dim)


def dot(a, b):
    return lax.dot_general(a, b, (((1,), (0,)), ((), ())), preferred_element_type=F32)


def dot_t(a, b):
    return lax.dot_general(a, b, (((1,), (1,)), ((), ())), preferred_element_type=F32)


def cos_sin(phase):
    quadrant = ((phase + 256) >> 9) & 3
    rest = (phase - 512 * ((phase + 256) >> 9)).astype(F32) * (2.0 * math.pi / 2048)
    square = rest * rest
    sine = rest * (1.0 + square * (-1.0 / 6 + square * (1.0 / 120 + square * (-1.0 / 5040 + square * (1.0 / 362880)))))
    cosine = 1.0 + square * (-0.5 + square * (1.0 / 24 + square * (-1.0 / 720 + square * (1.0 / 40320 - square * (1.0 / 3628800)))))
    odd = (quadrant & 1) == 1
    first, second = jnp.where(odd, sine, cosine), jnp.where(odd, cosine, sine)
    first = jnp.where((quadrant == 1) | (quadrant == 2), -first, first)
    second = jnp.where(quadrant >= 2, -second, second)
    return first, second


def kernel(bins_in, starts_in, traces, out, bins, starts, x_buf, table, tiles, send, received, field, left, blocks,
           load_sem, small_sem, send_sem, recv_sem, own_sem, ready_sem):
    f, r, y = (lax.axis_index(n) for n in ("freq", "row", "col"))
    x, zh, zl, core = f // 2, f % 2, r // 2, r % 2
    z = zh * 4 + zl

    def device(x, y, z, core):
        return (x * 2 + z // 4, z % 4 * 2 + core, y)

    barrier = pltpu.get_barrier_semaphore()

    def along_z(k):
        return device(x, y, (z + k // 2) % 8, (core + k % 2) % 2)

    def along_xy(k):
        return device((x + k // 4) % 4, (y + k % 4) % 4, z, core)

    for k in range(1, 16):
        pl.semaphore_signal(barrier, inc=1, device_id=along_z(k), device_id_type=MESH)
    for k in range(1, 16):
        pl.semaphore_signal(barrier, inc=1, device_id=along_xy(k), device_id_type=MESH)

    copy_bins = pltpu.make_async_copy(bins_in, bins, small_sem.at[0])
    copy_starts = pltpu.make_async_copy(starts_in, starts, small_sem.at[1])
    copy_bins.start()

    def load(n):
        return pltpu.make_async_copy(
            traces.at[n // 2, pl.ds(n % 2 * 512, 512)],
            x_buf.at[pl.ds(pl.multiple_of(n * 512, 512), 512)],
            load_sem.at[n],
        )

    for n in range(4):
        load(n).start()
    copy_starts.start()

    row, col = iota((256, 256), 0), iota((256, 256), 1)
    outward = (col == (row & 15) * 16 + ((row >> 4) & 1) * 8 + (row >> 5)).astype(BF16)
    inward = (
        col == ((row >> 1) & 7) * 32 + (row >> 7) * 16 + (row & 1) * 8 + ((row >> 4) & 7)
    ).astype(BF16)

    lane, sub = iota((8, 128), 1), iota((8, 128), 0)

    def build(q):
        half = (core + 1 + q // 2) % 2

        def body(b, _):
            value = jnp.zeros((8, 128), jnp.int32)
            for u in range(8):
                to_y = (y + q % 2 * 2 + u // 4) % 4
                value = jnp.where(sub == u, bins[b * 32 + half * 16 + to_y * 4 + u % 4], value)
            c0, s0 = cos_sin((value * lane) & 2047)
            c1, s1 = cos_sin(((value * lane) & 15) * 128)
            rows = pl.ds(pl.multiple_of(b * 16, 16), 16)
            for u in range(16):
                ca = jnp.broadcast_to(c1[:, u:u + 1], (8, 128))
                sa = jnp.broadcast_to(s1[:, u:u + 1], (8, 128))
                both = jnp.concatenate([c0 * ca - s0 * sa, -(s0 * ca + c0 * sa)], axis=0)
                table[rows, u * 128:(u + 1) * 128] = both.astype(BF16)
            return 0

        lax.fori_loop(0, 8, body, 0, unroll=2)

    def transform(n):
        part = x_buf[pl.ds(pl.multiple_of(n * 512, 512), 512), :]
        spectrum = (dot_t(table[...], part) * (1.0 / math.sqrt(2048))).astype(BF16)
        for u in range(4):
            for b in range(8):
                tiles[pl.ds(pl.multiple_of(n * 64 + u * 16, 16), 16), b * 128:(b + 1) * 128] = (
                    spectrum[b * 16:(b + 1) * 16, u * 128:(u + 1) * 128]
                )

    def pack(q):
        for n in range(4):
            part = dot(outward, tiles[:, n * 256:(n + 1) * 256]).astype(BF16)
            for u in range(2):
                for j in range(8):
                    send[q * 64 + n * 16 + u * 8 + j] = part[j * 32:(j + 1) * 32, u * 128:(u + 1) * 128]

    mine = y * 64 + r * 8 + f

    def spread(q, k):
        to_x, to_y = (x + (k // 8 % 4)) % 4, (y + q % 2 * 2 + (k // 32 % 2)) % 4
        to_z = (z + (k // 1 % 4) + (k // 4 % 2) * 4) % 8
        place = q * 64 + (to_x * 2 + to_z // 4) * 8 + (k // 32 % 2) * 4 + to_z % 4
        return place, device(to_x, to_y, to_z, (core + 1 + q // 2) % 2)

    def push(q):
        def body(k, _):
            place, target = spread(q, k)
            pltpu.make_async_remote_copy(
                src_ref=send.at[place], dst_ref=received.at[mine], send_sem=send_sem.at[0],
                recv_sem=recv_sem.at[q * 4 + (k // 1 % 4)], device_id=target, device_id_type=MESH,
            ).start()
            return 0

        lax.fori_loop(jnp.where(q == 2, 1, 0), 64, body, 0)

    copy_bins.wait()
    build(0)
    for n in range(1):
        load(n).wait()
        transform(n)
    pl.semaphore_wait(barrier, 30)

    for k in range(1, 16):
        pl.semaphore_signal(ready_sem, inc=1, device_id=along_xy(k), device_id_type=MESH)
    for n in range(1, 4):
        load(n).wait()
        transform(n)
    pack(0)
    pl.semaphore_wait(ready_sem, 15)
    push(0)

    def quarter(q, _):
        def body(n, _):
            transform(n)
            return 0

        build(q)
        lax.fori_loop(0, 4, body, 0)
        pack(q)
        push(q)
        return 0

    lax.fori_loop(1, 4, quarter, 0)
    place, _ = spread(2, 0)
    own = pltpu.make_async_copy(send.at[place], received.at[mine], own_sem.at[0])
    own.start()

    copy_starts.wait()
    lane = iota((16, 512), 1)
    weight = jnp.zeros((16, 512), F32)
    for n in range(8):
        weight = weight + jnp.where(lane >> 6 == starts[n], 1.0, 0.0)

    def unpack(g):
        q = g // 4
        from_r = (zl + 4 - g % 4) % 4 * 2 + (core + 1 + q // 2) % 2
        block = [(y + 8 - q % 2 * 2 - u) % 4 * 8 + from_r for u in range(2)]
        if g == 8:
            own.wait()
        arrived = received.at[pl.ds(0, 15 if g == 8 else 16)]
        pltpu.make_async_copy(arrived, arrived, recv_sem.at[g]).wait()
        part = jnp.concatenate(
            [received[pl.ds(block[u] * 8, 8)].reshape(256, 128) for u in range(2)], axis=1
        )
        part = dot(inward, part)
        for u in range(2):
            first = block[u] * 16
            upper, lower = pl.ds(pl.multiple_of(first, 16), 16), pl.ds(pl.multiple_of(512 + first, 16), 16)
            for c in range(2):
                for i in range(8):
                    value = part[(c * 8 + i) * 16:(c * 8 + i + 1) * 16, u * 128:(u + 1) * 128]
                    field[lower if c else upper, i * 128:(i + 1) * 128] = value.astype(BF16)
                    if i < 4:
                        value = value * weight[:, i * 128:(i + 1) * 128]
                        one, two = slice(i * 128, (i + 1) * 128), slice(512 + i * 128, 512 + (i + 1) * 128)
                        if c == 0:
                            left[upper, one] = value.astype(BF16)
                            left[lower, two] = value.astype(BF16)
                        else:
                            left[lower, one] = value.astype(BF16)
                            left[upper, two] = (-value).astype(BF16)

    for g in range(16):
        unpack(g)

    entry = core * 16 + y * 4 + zl

    def multiply(t):
        to_zl = jnp.where(t == 0, (zl + 2) % 4, jnp.where(t == 1, 3 - zl, jnp.where(t == 2, zl + 1 - zl % 2 * 2, zl)))
        lanes = pl.ds(pl.multiple_of(to_zl * 256, 256), 256)
        for part in range(4):
            c, pair = part // 2, (part + 1 + y // 2) % 2
            rows = pl.ds(pl.multiple_of(c * 512 + pair * 256, 256), 256)
            sums = dot(left[rows, :], field[:, lanes]) * (1.0 / math.sqrt(512))
            turned = sums.astype(BF16).T
            for to_core in range(2):
                for u in range(2):
                    blocks[t * 16 + c * 8 + to_core * 4 + pair * 2 + u] = (
                        turned[to_core * 128:(to_core + 1) * 128, u * 128:(u + 1) * 128]
                    )

            def body(k, _):
                to_core, to_y = k % 2, pair * 2 + k // 2

                @pl.when((t < 3) | (to_core != core) | (to_y != y))
                def _():
                    pltpu.make_async_remote_copy(
                        src_ref=blocks.at[t * 16 + c * 8 + to_core * 4 + to_y], dst_ref=out.at[c, entry],
                        send_sem=send_sem.at[1], recv_sem=recv_sem.at[16],
                        device_id=(f, to_zl * 2 + to_core, to_y), device_id_type=MESH,
                    ).start()

                return 0

            lax.fori_loop(0, 4, body, 0)

    def step(t, _):
        multiply(t)
        return 0

    lax.fori_loop(0, 3, step, 0)
    multiply(3)
    last = [
        pltpu.make_async_copy(blocks.at[48 + c * 8 + core * 4 + y], out.at[c, entry], own_sem.at[1 + c])
        for c in range(2)
    ]
    for c in range(2):
        last[c].start()

    sent = send.at[pl.ds(0, 255)]
    pltpu.make_async_copy(sent, sent, send_sem.at[0]).wait()
    for c in range(2):
        last[c].wait()
    sent = blocks.at[pl.ds(0, 62)]
    pltpu.make_async_copy(sent, sent, recv_sem.at[16]).wait()
    pltpu.make_async_copy(sent, sent, send_sem.at[1]).wait()


def on_device(traces, band_bins, panel_start):
    return pl.pallas_call(
        kernel,
        out_shape=jax.ShapeDtypeStruct((2, 32, 128, 128), BF16),
        in_specs=[
            pl.BlockSpec(memory_space=pl.ANY),
            pl.BlockSpec(memory_space=pl.ANY),
            pl.BlockSpec(memory_space=pl.ANY),
        ],
        out_specs=pl.BlockSpec(memory_space=pltpu.VMEM),
        scratch_shapes=[
            pltpu.SMEM((256,), jnp.int32),
            pltpu.SMEM((8,), jnp.int32),
            pltpu.VMEM((2048, 2048), BF16),
            pltpu.VMEM((128, 2048), BF16),
            pltpu.VMEM((256, 1024), BF16),
            pltpu.VMEM((256, 32, 128), BF16),
            pltpu.VMEM((256, 32, 128), BF16),
            pltpu.VMEM((1024, 1024), BF16),
            pltpu.VMEM((1024, 1024), BF16),
            pltpu.VMEM((64, 128, 128), BF16),
            pltpu.SemaphoreType.DMA((4,)),
            pltpu.SemaphoreType.DMA((2,)),
            pltpu.SemaphoreType.DMA((2,)),
            pltpu.SemaphoreType.DMA((17,)),
            pltpu.SemaphoreType.DMA((3,)),
            pltpu.SemaphoreType.REGULAR,
        ],
        compiler_params=pltpu.CompilerParams(
            collective_id=0, has_side_effects=True, vmem_limit_bytes=48 * 2**20
        ),
        cost_estimate=pl.CostEstimate(flops=9_000_000_000, bytes_accessed=10 * 2**20, transcendentals=0),
        name="multiples",
    )(*(pltpu.with_memory_space_constraint(v, pltpu.HBM) for v in (band_bins, panel_start, traces)))


def solution(mesh):
    return jax.shard_map(
        on_device,
        mesh=mesh,
        in_specs=(P(("col", "row", "freq"), None, None), P(), P()),
        out_specs=P(None, "freq", "row", "col"),
        check_vma=False,
    )
```
